32 devices in a mesh: row: 8 (over y, x, core), col: 4 (over z).
Axes of the slice: x: 2, y: 2, z: 4, core: 2. Of those that a mesh axis runs over, the one named last changes fastest.
Arguments:
- affiliation: bfloat16 [16384, 512], P(('row', 'col'))
- wanted_tiles: int32 [4, 8, 8], P('col', None, 'row'), may hold values from 0 to 3
- slot_peers: int32 [4, 8, 128], P('col', None, 'row'), may hold values from 0 to 7, as said below
- edge_words: int32 [4, 8, 16, 16384], P('col', None, None, 'row'), may hold values from 0 to 255, as said below
Outputs:
- affiliation_next: float32 [16384, 512], P(('row', 'col'))
The draws below stay inside these ranges and needn't reach their ends.
Inputs may be any that keep to these rules, and one draw needn't show every extreme that they name: `slot_peers`: the 8 entries of one column group and one row tile are distinct. `edge_words`: each word holds 8 mask bits.
All inputs are finite; a program needn't handle non-finite values.
Results may differ from the reference program's by a relative error of at most 0.0003.
Values may be sent and summed in bfloat16 or wider, within the bound.
A program may use at most 128 MiB of HBM per device.

```python
import math
import jax
import jax.numpy as jnp
from jax import lax

K = 512
TILE = 128
OWN = 4
NBR = 8
WORDS = 16
RANGE_TILES = 16
NODES = 16384
N_ROW = 8
N_COL = 4


def loguniform_draw(key, dims_shape, low_end, high_end):
    return jnp.exp(jax.random.uniform(key, dims_shape, jnp.float32, math.log(low_end), math.log(high_end)))


def draw_affiliation(key, part):
    key = jax.random.fold_in(key, 3)
    row_key, col_key, entry_key = jax.random.split(key, 3)
    node_trend = 1.0 + 2.0 * jnp.arange(NODES, dtype=jnp.float32)[:, None] / NODES
    row_scale = loguniform_draw(row_key, (NODES, 1), 0.2, 1.0)
    col_scale = loguniform_draw(col_key, (1, K), 0.5, 2.0)
    entries = jax.random.uniform(entry_key, (NODES, K), jnp.float32)
    return (node_trend * row_scale * col_scale * entries).astype(jnp.bfloat16)


def draw_slot_peers(key, part):
    key = jax.random.fold_in(key, 5)
    tiles_all = NODES // TILE
    scores = jax.random.randint(key, (N_COL, tiles_all, N_ROW), 0, 1 << 20)
    scores = scores * N_ROW + jnp.arange(N_ROW, dtype=jnp.int32)
    ranked = jnp.argsort(scores, axis=-1, stable=True)[..., :NBR]
    return jnp.transpose(ranked, (0, 2, 1)).astype(jnp.int32)


def draw_edge_words(key, part):
    key = jax.random.fold_in(key, 7)
    level_key, bit_key = jax.random.split(key)
    tiles_all = NODES // TILE
    density_level = jax.random.randint(level_key, (N_COL, NBR, 1, tiles_all, 1), 0, 3)
    mask_words = jnp.zeros((N_COL, NBR, WORDS, tiles_all, TILE), jnp.int32)
    for bit_place in range(8):
        bit_draws = jax.random.randint(jax.random.fold_in(bit_key, bit_place), mask_words.shape, 0, 8)
        mask_words = mask_words + jnp.where(bit_draws < 1 + 3 * density_level, 1 << bit_place, 0).astype(jnp.int32)
    return mask_words.reshape(N_COL, NBR, WORDS, NODES)


def with_ends(result, rng, least, top_value):
    shape = result.shape
    place = [jax.random.randint(jax.random.fold_in(rng, axis), (), 0, shape[axis]) for axis in range(len(shape))]
    result = result.at[tuple(place)].set(least)
    longest = shape.index(max(shape))
    place[longest] = (place[longest] + 1) % shape[longest]
    return result.at[tuple(place)].set(top_value)


def setup_inputs(seed: int = 0) -> dict:
    key_of = jax.random.split(jax.random.key(seed), 5)
    return {
        "affiliation": draw_affiliation(jax.random.fold_in(key_of[4], 71), 0),
        "wanted_tiles": with_ends(jax.random.randint(key_of[1], (N_COL, N_ROW, N_ROW), 0, OWN), jax.random.fold_in(key_of[1], 1), 0, OWN - 1).astype(jnp.int32),
        "slot_peers": draw_slot_peers(jax.random.fold_in(key_of[4], 71), 0),
        "edge_words": draw_edge_words(jax.random.fold_in(key_of[4], 71), 0),
    }


BACKGROUND = 0.25
NEG_RATE = 0.1
STEP_SIZE = 0.005


def unpack(mask_words):
    shifts = jnp.arange(8, dtype=jnp.int32)
    arc_bits = jnp.bitwise_and(jnp.right_shift(mask_words[..., :, None, :], shifts[:, None]), 1)
    return arc_bits.reshape(mask_words.shape[:-2] + (mask_words.shape[-2] * 8, mask_words.shape[-1]))


def reference(affiliation, wanted_tiles, slot_peers, edge_words):
    neg_weight = NEG_RATE * NBR * TILE / NODES
    tile_count = NODES // TILE
    node_tiles = affiliation.reshape(tile_count, TILE, K)
    column_sums = jnp.sum(affiliation.astype(jnp.float32), axis=0)
    group_index = jnp.arange(N_COL, dtype=jnp.int32)[:, None, None]
    range_index = (jnp.arange(tile_count, dtype=jnp.int32) // RANGE_TILES)[None, None, :]
    local_tile = wanted_tiles[group_index, slot_peers, range_index]
    col_tiles = ((slot_peers * N_COL + group_index) * OWN + local_tile).astype(jnp.int32)
    block_tiles = 4

    def one_block(first_tile):
        row_block = lax.dynamic_slice_in_dim(node_tiles, first_tile, block_tiles, 0).astype(jnp.float32)
        block_ids = lax.dynamic_slice_in_dim(col_tiles, first_tile, block_tiles, 2)
        col_block = node_tiles[block_ids].astype(jnp.float32)
        mask_words = lax.dynamic_slice_in_dim(edge_words, first_tile * TILE, block_tiles * TILE, 3)
        arc_bits = unpack(mask_words).reshape(N_COL, NBR, TILE, block_tiles, TILE).astype(jnp.float32)
        scores = jnp.einsum("cjbvk,buk->cjvbu", col_block, row_block) / K + BACKGROUND
        weights = (arc_bits * (1.0 / jnp.expm1(scores) + neg_weight)).astype(jnp.bfloat16)
        attract = jnp.einsum("cjvbu,cjbvk->buk", weights.astype(jnp.float32), col_block)
        return attract.reshape(block_tiles * TILE, K)

    attract = lax.map(one_block, jnp.arange(0, tile_count, block_tiles, dtype=jnp.int32))
    attract = attract.reshape(NODES, K)
    own_values = affiliation.astype(jnp.float32)
    gradient = attract - neg_weight * (column_sums[None, :] - own_values)
    return jnp.maximum(own_values + STEP_SIZE * gradient, 0.0)
```

```python
import functools
import math

import jax
import jax.numpy as jnp
from jax import lax
from jax.experimental import pallas as pl
from jax.experimental.pallas import tpu as pltpu
from jax.sharding import PartitionSpec as P

TILE = 128
NBR = 8
MESH = pl.DeviceIdType.MESH


BACKGROUND = 0.25
NEG_RATE = 0.1
STEP_SIZE = 0.005


def unpack(mask_words):
    shifts = jnp.arange(8, dtype=jnp.int32)
    arc_bits = jnp.bitwise_and(jnp.right_shift(mask_words[..., :, None, :], shifts[:, None]), 1)
    return arc_bits.reshape(
        mask_words.shape[:-2] + (mask_words.shape[-2] * 8, mask_words.shape[-1])
    )


def local(affiliation, wanted_tiles, slot_peers, edge_words):
    own_rows, community = affiliation.shape
    rows_axis = lax.axis_size("row")
    cols_axis = lax.axis_size("col")
    node_count = own_rows * rows_axis * cols_axis
    neg_weight = NEG_RATE * NBR * TILE / node_count
    own_tiles = own_rows // TILE
    range_rows = lax.all_gather(affiliation, "col", axis=0, tiled=True)
    requests = wanted_tiles.reshape(rows_axis)
    group_rows = lax.all_gather(affiliation, "row", axis=0, tiled=True)
    fetched = group_rows.reshape(rows_axis, own_tiles, TILE, community)[
        jnp.arange(rows_axis), requests
    ]
    column_sums = lax.psum(jnp.sum(affiliation, axis=0, dtype=jnp.float32), ("row", "col"))
    peer_table = slot_peers.reshape(NBR, -1)
    word_table = edge_words.reshape(NBR, TILE // 8, -1)
    row_tiles = range_rows.reshape(-1, TILE, community)
    row_count = own_rows * lax.axis_size("col")
    block_tiles = math.gcd(4, row_count // TILE)

    def one_block(block_index):
        start_tile = block_index * block_tiles
        row_block = lax.dynamic_slice_in_dim(row_tiles, start_tile, block_tiles, 0)
        peer_ids = lax.dynamic_slice_in_dim(peer_table, start_tile, block_tiles, 1)
        col_block = fetched[peer_ids]
        mask_words = lax.dynamic_slice_in_dim(word_table, start_tile * TILE, block_tiles * TILE, 2)
        arc_bits = unpack(mask_words).reshape(NBR, TILE, block_tiles, TILE).astype(jnp.float32)
        scores = (
            jnp.einsum("jbvk,buk->jvbu", col_block, row_block, preferred_element_type=jnp.float32)
            / community
            + BACKGROUND
        )
        weights = (arc_bits * (1.0 / jnp.expm1(scores) + neg_weight)).astype(jnp.bfloat16)
        attract = jnp.einsum(
            "jvbu,jbvk->buk", weights, col_block, preferred_element_type=jnp.float32
        )
        return attract.reshape(block_tiles * TILE, community)

    blocks_out = lax.map(one_block, jnp.arange(row_count // (block_tiles * TILE), dtype=jnp.int32))
    merged = lax.psum_scatter(
        blocks_out.reshape(row_count, community), "col", scatter_dimension=0, tiled=True
    )
    own_values = affiliation.astype(jnp.float32)
    gradient = merged - neg_weight * (column_sums[None, :] - own_values)
    return jnp.maximum(own_values + STEP_SIZE * gradient, 0.0)

def step_kernel(
    n_row, n_col, neg_weight,
    peers_ref, wanted_ref, own_ref, words_ref, out_ref,
    raw, stage, tiles, words_out, words_in, word_bits, weights, total,
    note, notes, line_note, line_notes,
    raw_send, raw_recv, tile_send, tile_recv, words_send, words_recv,
    note_send, note_recv, line_send, line_recv,
):
    own_rows, community = own_ref.shape
    own_tiles = own_rows // TILE
    lanes = community // 128
    p = lax.axis_index("row")
    c = lax.axis_index("col")

    def row_peer(k):
        return lax.rem(p + k, n_row)

    def col_peer(k):
        return lax.rem(c + k, n_col)

    def raw_copy(g, up):
        target = jnp.clip(c + 1, 0, n_col - 1) if up else jnp.maximum(c - 1, 0)
        return pltpu.make_async_remote_copy(
            src_ref=raw.at[g], dst_ref=raw.at[g],
            send_sem=raw_send.at[int(up), g], recv_sem=raw_recv.at[g],
            device_id=(p, target), device_id_type=MESH)

    def tile_copy(g, k, slot):
        return pltpu.make_async_remote_copy(
            src_ref=stage.at[g, k],
            dst_ref=tiles.at[g, pl.ds(pl.multiple_of(slot * TILE, TILE), TILE)],
            send_sem=tile_send.at[g, k], recv_sem=tile_recv.at[g, slot],
            device_id=(row_peer(k), c), device_id_type=MESH)

    def words_copy(k, slot):
        return pltpu.make_async_remote_copy(
            src_ref=words_out.at[k], dst_ref=words_in.at[slot],
            send_sem=words_send.at[k], recv_sem=words_recv.at[slot],
            device_id=(p, col_peer(k)), device_id_type=MESH)

    def note_copy(k, slot):
        return pltpu.make_async_remote_copy(
            src_ref=note, dst_ref=notes.at[slot],
            send_sem=note_send.at[k], recv_sem=note_recv.at[slot],
            device_id=(row_peer(k), c), device_id_type=MESH)

    def line_copy(k, slot):
        return pltpu.make_async_remote_copy(
            src_ref=line_note, dst_ref=line_notes.at[slot],
            send_sem=line_send.at[k], recv_sem=line_recv.at[slot],
            device_id=(p, col_peer(k)), device_id_type=MESH)

    def each(first, last, body):
        def step(i, carry):
            body(i)
            return carry
        lax.fori_loop(first, last, step, 0)

    barrier = pltpu.get_barrier_semaphore()
    for k in range(1, n_row):
        pl.semaphore_signal(barrier, inc=1, device_id=(row_peer(k), c), device_id_type=MESH)
    for k in range(1, n_col):
        pl.semaphore_signal(barrier, inc=1, device_id=(p, col_peer(k)), device_id_type=MESH)

    raw[c] = own_ref[...]
    total[...] = jnp.zeros_like(total)
    sums = jnp.sum(own_ref[...].astype(jnp.float32), axis=0, keepdims=True)
    note[...] = jnp.zeros_like(note)
    note[pl.ds(0, n_row), :] = wanted_ref[...].astype(jnp.float32)
    for i in range(lanes):
        note[pl.ds(n_row + i, 1), :] = sums[:, i * 128:(i + 1) * 128]
    notes[p] = note[...]
    pl.semaphore_wait(barrier, n_row - 1 + n_col - 1)

    each(1, n_row, lambda k: note_copy(k, p).start())
    pl.when(c + 1 < n_col)(lambda: raw_copy(c, True).start())
    pl.when(c > 0)(lambda: raw_copy(c, False).start())

    def order_words(k):
        b = col_peer(k)
        for t in range(own_tiles):
            at = b * own_tiles + t
            lane = pl.ds(pl.multiple_of(at * TILE, TILE), TILE)
            slot_words = [words_ref[j, :, lane] for j in range(NBR)]
            slot_peer = [peers_ref[j, at] for j in range(NBR)]
            for q in range(n_row):
                got = jnp.zeros((TILE // 8, TILE), jnp.int32)
                for j in range(NBR):
                    got = jnp.where(slot_peer[j] == q, slot_words[j], got)
                words_out[k, q * 16:(q + 1) * 16, t * TILE:(t + 1) * TILE] = (
                    got.astype(jnp.float32).astype(jnp.bfloat16))

    each(1, n_row, lambda k: note_copy(k, row_peer(k)).wait_recv())
    line_note[...] = jnp.sum(notes[...], axis=0)
    for r in range(n_row):
        line_note[pl.ds(r, 1), :] = notes[r, pl.ds(p, 1), :]
    line_notes[c] = line_note[...]
    each(1, n_col, lambda k: line_copy(k, c).start())

    def send_tiles(g):
        def one(k):
            r = row_peer(k)
            wanted = line_notes[g, pl.ds(r, 1), :]
            picks = [
                jnp.broadcast_to(
                    jnp.concatenate([jnp.where(wanted == i, 1.0, 0.0)] * lanes, axis=1),
                    (16, community)).astype(jnp.bfloat16)
                for i in range(own_tiles)]
            for q in range(TILE // 16):
                got = raw[g, q * 16:(q + 1) * 16, :] * picks[0]
                for i in range(1, own_tiles):
                    got = got + raw[g, i * TILE + q * 16:i * TILE + (q + 1) * 16, :] * picks[i]
                stage[g, k, q * 16:(q + 1) * 16, :] = got

        def send(k):
            one(k)
            tile_copy(g, k, p).start()

        each(1, n_row, send)
        one(0)
        tiles[g, pl.ds(pl.multiple_of(p * TILE, TILE), TILE), :] = stage[g, 0]

    chunk = math.gcd(4, n_row) * TILE
    bit_of_row = lax.shift_left(1, lax.broadcasted_iota(jnp.int32, (chunk // 8, 8, own_rows), 1))
    scale = math.log2(math.e)

    def compute(g):
        word_bits[...] = words_in[g].astype(jnp.float32).astype(jnp.int32)

        def part(i):
            rows = pl.ds(pl.multiple_of(i * chunk, chunk), chunk)
            scores = lax.dot_general(
                tiles[g, rows, :], own_ref[...], (((1,), (1,)), ((), ())),
                preferred_element_type=jnp.float32)
            grown = jnp.exp2(scores * (scale / community) + BACKGROUND * scale)
            value = 1.0 / (grown - 1.0) + neg_weight
            words = word_bits[pl.ds(pl.multiple_of(i * (chunk // 8), chunk // 8), chunk // 8), :]
            arcs = jnp.bitwise_and(
                jnp.broadcast_to(words[:, None, :], (chunk // 8, 8, own_rows)), bit_of_row)
            value = jnp.where(arcs.reshape(chunk, own_rows) != 0, value, 0.0)
            weights[rows, :] = value.astype(jnp.bfloat16)

        each(0, n_row * TILE // chunk, part)
        total[...] += lax.dot_general(
            weights[...], tiles[g], (((0,), (0,)), ((), ())),
            preferred_element_type=jnp.float32)

    send_tiles(c)
    each(0, n_col, order_words)
    words_in[c] = words_out[0]
    each(1, n_col, lambda k: words_copy(k, c).start())
    each(1, n_col, lambda k: line_copy(k, col_peer(k)).wait_recv())

    def sides(s, body):
        @pl.when(c - s >= 0)
        def _():
            body(c - s, True)

        @pl.when((s > 0) & (c + s < n_col))
        def _():
            body(c + s, False)

    def arrive(g, up):
        raw_copy(g, up).wait_recv()
        if up:
            pl.when(c + 1 < n_col)(lambda: raw_copy(g, True).start())
        else:
            pl.when(c > 0)(lambda: raw_copy(g, False).start())
        send_tiles(g)

    def use(g, up):
        each(1, n_row, lambda k: tile_copy(g, k, row_peer(k)).wait_recv())
        pl.when(g != c)(lambda: words_copy(1, g).wait_recv())
        compute(g)

    def step(s):
        sides(s, arrive)
        sides(s - 1, use)

    each(1, n_col + 1, step)

    sums_all = jnp.sum(line_notes[...], axis=0)
    for i in range(lanes):
        lane = slice(i * 128, (i + 1) * 128)
        own_values = own_ref[:, lane].astype(jnp.float32)
        gradient = total[:, lane] - neg_weight * (sums_all[n_row + i:n_row + i + 1, :] - own_values)
        out_ref[:, lane] = jnp.maximum(own_values + STEP_SIZE * gradient, 0.0)

    def sent(s):
        def one(g, up):
            if up:
                pl.when(c + 1 < n_col)(lambda: raw_copy(g, True).wait_send())
                pl.when((s == 0) & (c > 0))(lambda: raw_copy(g, False).wait_send())
            else:
                pl.when(c > 0)(lambda: raw_copy(g, False).wait_send())
            each(1, n_row, lambda k: tile_copy(g, k, p).wait_send())
        sides(s, one)

    each(0, n_col, sent)
    each(1, n_row, lambda k: note_copy(k, p).wait_send())
    each(1, n_col, lambda k: line_copy(k, c).wait_send())
    each(1, n_col, lambda k: words_copy(k, c).wait_send())


def fused(n_row, n_col, affiliation, wanted_tiles, slot_peers, edge_words):
    own_rows, community = affiliation.shape
    neg_weight = NEG_RATE * NBR * TILE / (own_rows * n_row * n_col)
    wanted = jnp.broadcast_to(wanted_tiles.reshape(n_row, 1), (n_row, 128))
    peers = slot_peers.reshape(NBR, -1)
    words = edge_words.reshape(NBR, TILE // 8, -1)
    note_rows = -(-(n_row + community // 128) // 8) * 8
    dense = n_row * TILE
    dma = pltpu.SemaphoreType.DMA
    vmem = pl.BlockSpec(memory_space=pltpu.VMEM)
    return pl.pallas_call(
        functools.partial(step_kernel, n_row, n_col, neg_weight),
        out_shape=jax.ShapeDtypeStruct((own_rows, community), jnp.float32),
        in_specs=[pl.BlockSpec(memory_space=pltpu.SMEM), vmem, vmem, vmem],
        out_specs=vmem,
        scratch_shapes=[
            pltpu.VMEM((n_col, own_rows, community), jnp.bfloat16),
            pltpu.VMEM((n_col, n_row, TILE, community), jnp.bfloat16),
            pltpu.VMEM((n_col, dense, community), jnp.bfloat16),
            pltpu.VMEM((n_col, dense // 8, own_rows), jnp.bfloat16),
            pltpu.VMEM((n_col, dense // 8, own_rows), jnp.bfloat16),
            pltpu.VMEM((dense // 8, own_rows), jnp.int32),
            pltpu.VMEM((dense, own_rows), jnp.bfloat16),
            pltpu.VMEM((own_rows, community), jnp.float32),
            pltpu.VMEM((note_rows, 128), jnp.float32),
            pltpu.VMEM((n_row, note_rows, 128), jnp.float32),
            pltpu.VMEM((note_rows, 128), jnp.float32),
            pltpu.VMEM((n_col, note_rows, 128), jnp.float32),
            dma((2, n_col)), dma((n_col,)),
            dma((n_col, n_row)), dma((n_col, n_row)),
            dma((n_col,)), dma((n_col,)),
            dma((n_row,)), dma((n_row,)),
            dma((n_col,)), dma((n_col,)),
        ],
        compiler_params=pltpu.CompilerParams(
            collective_id=0, has_side_effects=True, vmem_limit_bytes=56 * 2**20),
    )(peers, wanted, affiliation, words)


def fits(n_row, n_col, own_rows, community):
    tile_bytes = 2 * TILE * community * 2 * n_row * n_col
    return tile_bytes + 2 * own_rows * community * n_col < 16 * 2**20


def solution(mesh):
    n_row, n_col = mesh.shape["row"], mesh.shape["col"]

    def part(affiliation, *rest):
        if fits(n_row, n_col, *affiliation.shape):
            return fused(n_row, n_col, affiliation, *rest)
        return local(affiliation, *rest)

    in_specs = (
        P(("row", "col"), None),
        P("col", None, "row"),
        P("col", None, "row"),
        P("col", None, None, "row"),
    )
    out_specs = P(("row", "col"), None)
    return jax.shard_map(part, mesh=mesh, in_specs=in_specs, out_specs=out_specs, check_vma=False)
```

```python
import functools
import math

import jax
import jax.numpy as jnp
from jax import lax
from jax.experimental import pallas as pl
from jax.experimental.pallas import tpu as pltpu
from jax.sharding import PartitionSpec as P

TILE = 128
NBR = 8
PIECES = 2
MESH = pl.DeviceIdType.MESH


BACKGROUND = 0.25
NEG_RATE = 0.1
STEP_SIZE = 0.005


def unpack(mask_words):
    shifts = jnp.arange(8, dtype=jnp.int32)
    arc_bits = jnp.bitwise_and(jnp.right_shift(mask_words[..., :, None, :], shifts[:, None]), 1)
    return arc_bits.reshape(
        mask_words.shape[:-2] + (mask_words.shape[-2] * 8, mask_words.shape[-1])
    )


def local(affiliation, wanted_tiles, slot_peers, edge_words):
    own_rows, community = affiliation.shape
    rows_axis = lax.axis_size("row")
    cols_axis = lax.axis_size("col")
    node_count = own_rows * rows_axis * cols_axis
    neg_weight = NEG_RATE * NBR * TILE / node_count
    own_tiles = own_rows // TILE
    range_rows = lax.all_gather(affiliation, "col", axis=0, tiled=True)
    requests = wanted_tiles.reshape(rows_axis)
    group_rows = lax.all_gather(affiliation, "row", axis=0, tiled=True)
    fetched = group_rows.reshape(rows_axis, own_tiles, TILE, community)[
        jnp.arange(rows_axis), requests
    ]
    column_sums = lax.psum(jnp.sum(affiliation, axis=0, dtype=jnp.float32), ("row", "col"))
    peer_table = slot_peers.reshape(NBR, -1)
    word_table = edge_words.reshape(NBR, TILE // 8, -1)
    row_tiles = range_rows.reshape(-1, TILE, community)
    row_count = own_rows * lax.axis_size("col")
    block_tiles = math.gcd(4, row_count // TILE)

    def one_block(block_index):
        start_tile = block_index * block_tiles
        row_block = lax.dynamic_slice_in_dim(row_tiles, start_tile, block_tiles, 0)
        peer_ids = lax.dynamic_slice_in_dim(peer_table, start_tile, block_tiles, 1)
        col_block = fetched[peer_ids]
        mask_words = lax.dynamic_slice_in_dim(word_table, start_tile * TILE, block_tiles * TILE, 2)
        arc_bits = unpack(mask_words).reshape(NBR, TILE, block_tiles, TILE).astype(jnp.float32)
        scores = (
            jnp.einsum("jbvk,buk->jvbu", col_block, row_block, preferred_element_type=jnp.float32)
            / community
            + BACKGROUND
        )
        weights = (arc_bits * (1.0 / jnp.expm1(scores) + neg_weight)).astype(jnp.bfloat16)
        attract = jnp.einsum(
            "jvbu,jbvk->buk", weights, col_block, preferred_element_type=jnp.float32
        )
        return attract.reshape(block_tiles * TILE, community)

    blocks_out = lax.map(one_block, jnp.arange(row_count // (block_tiles * TILE), dtype=jnp.int32))
    merged = lax.psum_scatter(
        blocks_out.reshape(row_count, community), "col", scatter_dimension=0, tiled=True
    )
    own_values = affiliation.astype(jnp.float32)
    gradient = merged - neg_weight * (column_sums[None, :] - own_values)
    return jnp.maximum(own_values + STEP_SIZE * gradient, 0.0)

def step_kernel(
    n_row, n_col, neg_weight,
    peers_ref, wanted_ref, own_ref, words_ref, out_ref,
    raw, stage, tiles, words_out, words_in, word_bits, weights, total,
    note, notes, line_note, line_notes,
    raw_send, raw_recv, tile_send, tile_recv, words_send, words_recv,
    note_send, note_recv, line_send, line_recv,
):
    own_rows, community = own_ref.shape
    own_tiles = own_rows // TILE
    lanes = community // 128
    width = community // PIECES
    p = lax.axis_index("row")
    c = lax.axis_index("col")

    def row_peer(k):
        return lax.rem(p + k, n_row)

    def col_peer(k):
        return lax.rem(c + k, n_col)

    def piece(q):
        return pl.ds(pl.multiple_of(q * width, width), width)

    def raw_copy(g, up, q):
        target = jnp.clip(c + 1, 0, n_col - 1) if up else jnp.maximum(c - 1, 0)
        return pltpu.make_async_remote_copy(
            src_ref=raw.at[g, :, piece(q)], dst_ref=raw.at[g, :, piece(q)],
            send_sem=raw_send.at[int(up), g, q], recv_sem=raw_recv.at[g, q],
            device_id=(p, target), device_id_type=MESH)

    def tile_copy(g, k, slot, q):
        return pltpu.make_async_remote_copy(
            src_ref=stage.at[g, k, :, piece(q)],
            dst_ref=tiles.at[g, pl.ds(pl.multiple_of(slot * TILE, TILE), TILE), piece(q)],
            send_sem=tile_send.at[g, q, k], recv_sem=tile_recv.at[g, q, slot],
            device_id=(row_peer(k), c), device_id_type=MESH)

    def words_copy(k, slot):
        return pltpu.make_async_remote_copy(
            src_ref=words_out.at[k], dst_ref=words_in.at[slot],
            send_sem=words_send.at[k], recv_sem=words_recv.at[slot],
            device_id=(p, col_peer(k)), device_id_type=MESH)

    def note_copy(k, slot):
        return pltpu.make_async_remote_copy(
            src_ref=note, dst_ref=notes.at[slot],
            send_sem=note_send.at[k], recv_sem=note_recv.at[slot],
            device_id=(row_peer(k), c), device_id_type=MESH)

    def line_copy(k, slot):
        return pltpu.make_async_remote_copy(
            src_ref=line_note, dst_ref=line_notes.at[slot],
            send_sem=line_send.at[k], recv_sem=line_recv.at[slot],
            device_id=(p, col_peer(k)), device_id_type=MESH)

    def each(first, last, body):
        def step(i, carry):
            body(i)
            return carry
        lax.fori_loop(first, last, step, 0)

    barrier = pltpu.get_barrier_semaphore()
    for k in range(1, n_row):
        pl.semaphore_signal(barrier, inc=1, device_id=(row_peer(k), c), device_id_type=MESH)
    for k in range(1, n_col):
        pl.semaphore_signal(barrier, inc=1, device_id=(p, col_peer(k)), device_id_type=MESH)

    raw[c] = own_ref[...]
    total[...] = jnp.zeros_like(total)
    sums = jnp.sum(own_ref[...].astype(jnp.float32), axis=0, keepdims=True)
    note[...] = jnp.zeros_like(note)
    note[pl.ds(0, n_row), :] = jnp.broadcast_to(wanted_ref[...], (n_row, 128)).astype(jnp.float32)
    for i in range(lanes):
        note[pl.ds(n_row + i, 1), :] = sums[:, i * 128:(i + 1) * 128]
    notes[p] = note[...]
    pl.semaphore_wait(barrier, n_row - 1 + n_col - 1)

    each(1, n_row, lambda k: note_copy(k, p).start())

    def send_own(q):
        pl.when(c + 1 < n_col)(lambda: raw_copy(c, True, q).start())
        pl.when(c > 0)(lambda: raw_copy(c, False, q).start())

    each(0, PIECES, send_own)

    def order_words(k):
        b = col_peer(k)
        for t in range(own_tiles):
            at = b * own_tiles + t
            lane = pl.ds(pl.multiple_of(at * TILE, TILE), TILE)
            slot_words = [words_ref[j, :, lane] for j in range(NBR)]
            slot_peer = [peers_ref[j, at] for j in range(NBR)]
            for q in range(n_row):
                got = jnp.zeros((TILE // 8, TILE), jnp.int32)
                for j in range(NBR):
                    got = jnp.where(slot_peer[j] == q, slot_words[j], got)
                words_out[k, q * 16:(q + 1) * 16, t * TILE:(t + 1) * TILE] = (
                    got.astype(jnp.float32).astype(jnp.bfloat16))

    each(1, n_row, lambda k: note_copy(k, row_peer(k)).wait_recv())
    line_note[...] = jnp.sum(notes[...], axis=0)
    for r in range(n_row):
        line_note[pl.ds(r, 1), :] = notes[r, pl.ds(p, 1), :]
    line_notes[c] = line_note[...]
    each(1, n_col, lambda k: line_copy(k, c).start())

    def send_tiles(g, q):
        def pick(k):
            r = row_peer(k)
            wanted = line_notes[g, pl.ds(r, 1), :]
            picks = [
                jnp.broadcast_to(
                    jnp.concatenate([jnp.where(wanted == i, 1.0, 0.0)] * (width // 128), axis=1),
                    (16, width)).astype(jnp.bfloat16)
                for i in range(own_tiles)]
            for h in range(TILE // 16):
                got = raw[g, h * 16:(h + 1) * 16, piece(q)] * picks[0]
                for i in range(1, own_tiles):
                    got = got + raw[g, i * TILE + h * 16:i * TILE + (h + 1) * 16, piece(q)] * picks[i]
                stage[g, k, h * 16:(h + 1) * 16, piece(q)] = got

        def send(k):
            pick(k)
            tile_copy(g, k, p, q).start()

        each(1, n_row, send)
        pick(0)
        tiles[g, pl.ds(pl.multiple_of(p * TILE, TILE), TILE), piece(q)] = stage[g, 0, :, piece(q)]

    chunk = math.gcd(4, n_row) * TILE
    bit_of_row = lax.shift_left(1, lax.broadcasted_iota(jnp.int32, (chunk // 8, 8, own_rows), 1))
    scale = math.log2(math.e)

    def compute(g):
        word_bits[...] = words_in[g].astype(jnp.float32).astype(jnp.int32)

        def part(i):
            rows = pl.ds(pl.multiple_of(i * chunk, chunk), chunk)
            scores = lax.dot_general(
                tiles[g, rows, :], own_ref[...], (((1,), (1,)), ((), ())),
                preferred_element_type=jnp.float32)
            grown = jnp.exp2(scores * (scale / community) + BACKGROUND * scale)
            value = 1.0 / (grown - 1.0) + neg_weight
            words = word_bits[pl.ds(pl.multiple_of(i * (chunk // 8), chunk // 8), chunk // 8), :]
            arcs = jnp.bitwise_and(
                jnp.broadcast_to(words[:, None, :], (chunk // 8, 8, own_rows)), bit_of_row)
            value = jnp.where(arcs.reshape(chunk, own_rows) != 0, value, 0.0)
            weights[rows, :] = value.astype(jnp.bfloat16)

        each(0, n_row * TILE // chunk, part)
        total[...] += lax.dot_general(
            weights[...], tiles[g], (((0,), (0,)), ((), ())),
            preferred_element_type=jnp.float32)

    each(0, PIECES, lambda q: send_tiles(c, q))
    each(0, n_col, order_words)
    words_in[c] = words_out[0]
    each(1, n_col, lambda k: words_copy(k, c).start())
    each(1, n_col, lambda k: line_copy(k, col_peer(k)).wait_recv())

    def sides(s, body):
        @pl.when(c - s >= 0)
        def _():
            body(c - s, True)

        @pl.when((s > 0) & (c + s < n_col))
        def _():
            body(c + s, False)

    def arrive(g, up, q):
        raw_copy(g, up, q).wait_recv()
        if up:
            pl.when(c + 1 < n_col)(lambda: raw_copy(g, True, q).start())
        else:
            pl.when(c > 0)(lambda: raw_copy(g, False, q).start())
        send_tiles(g, q)

    def use(g, up):
        each(0, PIECES, lambda q: each(
            1, n_row, lambda k: tile_copy(g, k, row_peer(k), q).wait_recv()))
        pl.when(g != c)(lambda: words_copy(1, g).wait_recv())
        compute(g)

    def step(s):
        each(0, PIECES, lambda q: sides(s, lambda g, up: arrive(g, up, q)))
        sides(s - 1, use)

    each(1, n_col + 1, step)

    sums_all = jnp.sum(line_notes[...], axis=0)
    for i in range(lanes):
        lane = slice(i * 128, (i + 1) * 128)
        own_values = own_ref[:, lane].astype(jnp.float32)
        gradient = total[:, lane] - neg_weight * (sums_all[n_row + i:n_row + i + 1, :] - own_values)
        out_ref[:, lane] = jnp.maximum(own_values + STEP_SIZE * gradient, 0.0)

    def sent(s):
        def one(g, up, q):
            if up:
                pl.when(c + 1 < n_col)(lambda: raw_copy(g, True, q).wait_send())
                pl.when((s == 0) & (c > 0))(lambda: raw_copy(g, False, q).wait_send())
            else:
                pl.when(c > 0)(lambda: raw_copy(g, False, q).wait_send())
            each(1, n_row, lambda k: tile_copy(g, k, p, q).wait_send())
        each(0, PIECES, lambda q: sides(s, lambda g, up: one(g, up, q)))

    each(0, n_col, sent)
    each(1, n_row, lambda k: note_copy(k, p).wait_send())
    each(1, n_col, lambda k: line_copy(k, c).wait_send())
    each(1, n_col, lambda k: words_copy(k, c).wait_send())


def fused(n_row, n_col, affiliation, wanted_tiles, slot_peers, edge_words):
    own_rows, community = affiliation.shape
    neg_weight = NEG_RATE * NBR * TILE / (own_rows * n_row * n_col)
    wanted = wanted_tiles.reshape(n_row, 1)
    peers = slot_peers.reshape(NBR, -1)
    words = edge_words.reshape(NBR, TILE // 8, -1)
    note_rows = -(-(n_row + community // 128) // 8) * 8
    dense = n_row * TILE
    dma = pltpu.SemaphoreType.DMA
    vmem = pl.BlockSpec(memory_space=pltpu.VMEM)
    return pl.pallas_call(
        functools.partial(step_kernel, n_row, n_col, neg_weight),
        out_shape=jax.ShapeDtypeStruct((own_rows, community), jnp.float32),
        in_specs=[pl.BlockSpec(memory_space=pltpu.SMEM), vmem, vmem, vmem],
        out_specs=vmem,
        scratch_shapes=[
            pltpu.VMEM((n_col, own_rows, community), jnp.bfloat16),
            pltpu.VMEM((n_col, n_row, TILE, community), jnp.bfloat16),
            pltpu.VMEM((n_col, dense, community), jnp.bfloat16),
            pltpu.VMEM((n_col, dense // 8, own_rows), jnp.bfloat16),
            pltpu.VMEM((n_col, dense // 8, own_rows), jnp.bfloat16),
            pltpu.VMEM((dense // 8, own_rows), jnp.int32),
            pltpu.VMEM((dense, own_rows), jnp.bfloat16),
            pltpu.VMEM((own_rows, community), jnp.float32),
            pltpu.VMEM((note_rows, 128), jnp.float32),
            pltpu.VMEM((n_row, note_rows, 128), jnp.float32),
            pltpu.VMEM((note_rows, 128), jnp.float32),
            pltpu.VMEM((n_col, note_rows, 128), jnp.float32),
            dma((2, n_col, PIECES)), dma((n_col, PIECES)),
            dma((n_col, PIECES, n_row)), dma((n_col, PIECES, n_row)),
            dma((n_col,)), dma((n_col,)),
            dma((n_row,)), dma((n_row,)),
            dma((n_col,)), dma((n_col,)),
        ],
        compiler_params=pltpu.CompilerParams(
            collective_id=0, has_side_effects=True, vmem_limit_bytes=56 * 2**20),
    )(peers, wanted, affiliation, words)


def fits(n_row, n_col, own_rows, community):
    tile_bytes = 2 * TILE * community * 2 * n_row * n_col
    return tile_bytes + 2 * own_rows * community * n_col < 16 * 2**20


def solution(mesh):
    n_row, n_col = mesh.shape["row"], mesh.shape["col"]

    def part(affiliation, *rest):
        if fits(n_row, n_col, *affiliation.shape):
            return fused(n_row, n_col, affiliation, *rest)
        return local(affiliation, *rest)

    in_specs = (
        P(("row", "col"), None),
        P("col", None, "row"),
        P("col", None, "row"),
        P("col", None, None, "row"),
    )
    out_specs = P(("row", "col"), None)
    return jax.shard_map(part, mesh=mesh, in_specs=in_specs, out_specs=out_specs, check_vma=False)
```

```python
import functools
import math

import jax
import jax.numpy as jnp
from jax import lax
from jax.experimental import pallas as pl
from jax.experimental.pallas import tpu as pltpu
from jax.sharding import PartitionSpec as P

TILE = 128
NBR = 8
PIECES = 2
MESH = pl.DeviceIdType.MESH


BACKGROUND = 0.25
NEG_RATE = 0.1
STEP_SIZE = 0.005


def unpack(mask_words):
    shifts = jnp.arange(8, dtype=jnp.int32)
    arc_bits = jnp.bitwise_and(jnp.right_shift(mask_words[..., :, None, :], shifts[:, None]), 1)
    return arc_bits.reshape(
        mask_words.shape[:-2] + (mask_words.shape[-2] * 8, mask_words.shape[-1])
    )


def local(affiliation, wanted_tiles, slot_peers, edge_words):
    own_rows, community = affiliation.shape
    rows_axis = lax.axis_size("row")
    cols_axis = lax.axis_size("col")
    node_count = own_rows * rows_axis * cols_axis
    neg_weight = NEG_RATE * NBR * TILE / node_count
    own_tiles = own_rows // TILE
    range_rows = lax.all_gather(affiliation, "col", axis=0, tiled=True)
    requests = wanted_tiles.reshape(rows_axis)
    group_rows = lax.all_gather(affiliation, "row", axis=0, tiled=True)
    fetched = group_rows.reshape(rows_axis, own_tiles, TILE, community)[
        jnp.arange(rows_axis), requests
    ]
    column_sums = lax.psum(jnp.sum(affiliation, axis=0, dtype=jnp.float32), ("row", "col"))
    peer_table = slot_peers.reshape(NBR, -1)
    word_table = edge_words.reshape(NBR, TILE // 8, -1)
    row_tiles = range_rows.reshape(-1, TILE, community)
    row_count = own_rows * lax.axis_size("col")
    block_tiles = math.gcd(4, row_count // TILE)

    def one_block(block_index):
        start_tile = block_index * block_tiles
        row_block = lax.dynamic_slice_in_dim(row_tiles, start_tile, block_tiles, 0)
        peer_ids = lax.dynamic_slice_in_dim(peer_table, start_tile, block_tiles, 1)
        col_block = fetched[peer_ids]
        mask_words = lax.dynamic_slice_in_dim(word_table, start_tile * TILE, block_tiles * TILE, 2)
        arc_bits = unpack(mask_words).reshape(NBR, TILE, block_tiles, TILE).astype(jnp.float32)
        scores = (
            jnp.einsum("jbvk,buk->jvbu", col_block, row_block, preferred_element_type=jnp.float32)
            / community
            + BACKGROUND
        )
        weights = (arc_bits * (1.0 / jnp.expm1(scores) + neg_weight)).astype(jnp.bfloat16)
        attract = jnp.einsum(
            "jvbu,jbvk->buk", weights, col_block, preferred_element_type=jnp.float32
        )
        return attract.reshape(block_tiles * TILE, community)

    blocks_out = lax.map(one_block, jnp.arange(row_count // (block_tiles * TILE), dtype=jnp.int32))
    merged = lax.psum_scatter(
        blocks_out.reshape(row_count, community), "col", scatter_dimension=0, tiled=True
    )
    own_values = affiliation.astype(jnp.float32)
    gradient = merged - neg_weight * (column_sums[None, :] - own_values)
    return jnp.maximum(own_values + STEP_SIZE * gradient, 0.0)

def step_kernel(
    n_row, n_col, neg_weight,
    peers_ref, wanted_ref, own_ref, words_ref, out_ref,
    raw, stage, tiles, words_out, words_in, word_bits, weights, total,
    note, notes, line_note, line_notes,
    raw_send, raw_recv, tile_send, tile_recv, words_send, words_recv,
    note_send, note_recv, line_send, line_recv,
):
    own_rows, community = own_ref.shape
    own_tiles = own_rows // TILE
    lanes = community // 128
    width = community // PIECES
    p = lax.axis_index("row")
    c = lax.axis_index("col")

    def row_peer(k):
        far = lax.rem(n_row - k, n_row)
        peer = 0
        bit = 1
        while bit < n_row:
            peer = peer + lax.rem(lax.div(p, bit) + lax.div(far, bit), 2) * bit
            bit *= 2
        return peer

    def col_peer(k):
        return lax.rem(c + k, n_col)

    def raw_copy(g, up, q):
        target = jnp.clip(c + 1, 0, n_col - 1) if up else jnp.maximum(c - 1, 0)
        return pltpu.make_async_remote_copy(
            src_ref=raw.at[g, q], dst_ref=raw.at[g, q],
            send_sem=raw_send.at[int(up), g, q], recv_sem=raw_recv.at[g, q],
            device_id=(p, target), device_id_type=MESH)

    def tile_copy(g, k, slot, q):
        return pltpu.make_async_remote_copy(
            src_ref=stage.at[g, q, k],
            dst_ref=tiles.at[g, q, pl.ds(pl.multiple_of(slot * TILE, TILE), TILE)],
            send_sem=tile_send.at[g, q, k], recv_sem=tile_recv.at[g, q, slot],
            device_id=(row_peer(k), c), device_id_type=MESH)

    def words_copy(k, slot):
        return pltpu.make_async_remote_copy(
            src_ref=words_out.at[k], dst_ref=words_in.at[slot],
            send_sem=words_send.at[k], recv_sem=words_recv.at[slot],
            device_id=(p, col_peer(k)), device_id_type=MESH)

    def note_copy(k, slot):
        return pltpu.make_async_remote_copy(
            src_ref=note, dst_ref=notes.at[slot],
            send_sem=note_send.at[k], recv_sem=note_recv.at[slot],
            device_id=(row_peer(k), c), device_id_type=MESH)

    def line_copy(k, slot):
        return pltpu.make_async_remote_copy(
            src_ref=line_note, dst_ref=line_notes.at[slot],
            send_sem=line_send.at[k], recv_sem=line_recv.at[slot],
            device_id=(p, col_peer(k)), device_id_type=MESH)

    def each(first, last, body):
        def step(i, carry):
            body(i)
            return carry
        lax.fori_loop(first, last, step, 0)

    barrier = pltpu.get_barrier_semaphore()
    for k in range(1, n_row):
        pl.semaphore_signal(barrier, inc=1, device_id=(row_peer(k), c), device_id_type=MESH)
    for k in range(1, n_col):
        pl.semaphore_signal(barrier, inc=1, device_id=(p, col_peer(k)), device_id_type=MESH)

    for q in range(PIECES):
        raw[c, q] = own_ref[:, q * width:(q + 1) * width]
    total[...] = jnp.zeros_like(total)
    sums = jnp.sum(own_ref[...].astype(jnp.float32), axis=0, keepdims=True)
    note[...] = jnp.zeros_like(note)
    note[pl.ds(0, n_row), :] = jnp.broadcast_to(wanted_ref[...], (n_row, 128)).astype(jnp.float32)
    for i in range(lanes):
        note[pl.ds(n_row + i, 1), :] = sums[:, i * 128:(i + 1) * 128]
    notes[p] = note[...]
    pl.semaphore_wait(barrier, n_row - 1 + n_col - 1)

    each(1, n_row, lambda k: note_copy(k, p).start())

    def send_own(q):
        pl.when(c + 1 < n_col)(lambda: raw_copy(c, True, q).start())
        pl.when(c > 0)(lambda: raw_copy(c, False, q).start())

    each(0, PIECES, send_own)

    def order_words(k):
        b = col_peer(k)
        for t in range(own_tiles):
            at = b * own_tiles + t
            lane = pl.ds(pl.multiple_of(at * TILE, TILE), TILE)
            slot_words = [words_ref[j, :, lane] for j in range(NBR)]
            slot_peer = [peers_ref[j, at] for j in range(NBR)]
            for q in range(n_row):
                got = jnp.zeros((TILE // 8, TILE), jnp.int32)
                for j in range(NBR):
                    got = jnp.where(slot_peer[j] == q, slot_words[j], got)
                words_out[k, q * 16:(q + 1) * 16, t * TILE:(t + 1) * TILE] = (
                    got.astype(jnp.float32).astype(jnp.bfloat16))

    each(1, n_row, lambda k: note_copy(k, row_peer(k)).wait_recv())
    line_note[...] = jnp.sum(notes[...], axis=0)
    for r in range(n_row):
        line_note[pl.ds(r, 1), :] = notes[r, pl.ds(p, 1), :]
    line_notes[c] = line_note[...]
    each(1, n_col, lambda k: line_copy(k, c).start())

    def send_tiles(g, q):
        def pick(k):
            r = row_peer(k)
            wanted = line_notes[g, pl.ds(r, 1), :]
            picks = [
                jnp.broadcast_to(
                    jnp.concatenate([jnp.where(wanted == i, 1.0, 0.0)] * (width // 128), axis=1),
                    (16, width)).astype(jnp.bfloat16)
                for i in range(own_tiles)]
            for h in range(TILE // 16):
                got = raw[g, q, h * 16:(h + 1) * 16, :] * picks[0]
                for i in range(1, own_tiles):
                    got = got + raw[g, q, i * TILE + h * 16:i * TILE + (h + 1) * 16, :] * picks[i]
                stage[g, q, k, h * 16:(h + 1) * 16, :] = got

        def send(k):
            pick(k)
            tile_copy(g, k, p, q).start()

        each(1, n_row, send)
        pick(0)
        tiles[g, q, pl.ds(pl.multiple_of(p * TILE, TILE), TILE), :] = stage[g, q, 0]

    chunk = math.gcd(4, n_row) * TILE
    bit_of_row = lax.shift_left(1, lax.broadcasted_iota(jnp.int32, (chunk // 8, 8, own_rows), 1))
    scale = math.log2(math.e)

    def compute(g):
        word_bits[...] = words_in[g].astype(jnp.float32).astype(jnp.int32)

        def part(i):
            rows = pl.ds(pl.multiple_of(i * chunk, chunk), chunk)
            scores = sum(
                lax.dot_general(
                    tiles[g, q, rows, :], raw[c, q], (((1,), (1,)), ((), ())),
                    preferred_element_type=jnp.float32)
                for q in range(PIECES))
            grown = jnp.exp2(scores * (scale / community) + BACKGROUND * scale)
            value = 1.0 / (grown - 1.0) + neg_weight
            words = word_bits[pl.ds(pl.multiple_of(i * (chunk // 8), chunk // 8), chunk // 8), :]
            arcs = jnp.bitwise_and(
                jnp.broadcast_to(words[:, None, :], (chunk // 8, 8, own_rows)), bit_of_row)
            value = jnp.where(arcs.reshape(chunk, own_rows) != 0, value, 0.0)
            weights[rows, :] = value.astype(jnp.bfloat16)

        each(0, n_row * TILE // chunk, part)
        for q in range(PIECES):
            total[:, q * width:(q + 1) * width] += lax.dot_general(
                weights[...], tiles[g, q], (((0,), (0,)), ((), ())),
                preferred_element_type=jnp.float32)

    each(0, PIECES, lambda q: send_tiles(c, q))
    each(0, n_col, order_words)
    words_in[c] = words_out[0]
    each(1, n_col, lambda k: words_copy(k, c).start())
    each(1, n_col, lambda k: line_copy(k, col_peer(k)).wait_recv())

    def sides(s, body):
        @pl.when(c - s >= 0)
        def _():
            body(c - s, True)

        @pl.when((s > 0) & (c + s < n_col))
        def _():
            body(c + s, False)

    def arrive(g, up, q):
        raw_copy(g, up, q).wait_recv()
        if up:
            pl.when(c + 1 < n_col)(lambda: raw_copy(g, True, q).start())
        else:
            pl.when(c > 0)(lambda: raw_copy(g, False, q).start())
        send_tiles(g, q)

    def use(g, up):
        each(0, PIECES, lambda q: each(
            1, n_row, lambda k: tile_copy(g, k, row_peer(k), q).wait_recv()))
        pl.when(g != c)(lambda: words_copy(1, g).wait_recv())
        compute(g)

    def step(s):
        each(0, PIECES, lambda q: sides(s, lambda g, up: arrive(g, up, q)))
        sides(s - 1, use)

    each(1, n_col + 1, step)

    sums_all = jnp.sum(line_notes[...], axis=0)
    for i in range(lanes):
        lane = slice(i * 128, (i + 1) * 128)
        own_values = own_ref[:, lane].astype(jnp.float32)
        gradient = total[:, lane] - neg_weight * (sums_all[n_row + i:n_row + i + 1, :] - own_values)
        out_ref[:, lane] = jnp.maximum(own_values + STEP_SIZE * gradient, 0.0)

    def sent(s):
        def one(g, up, q):
            if up:
                pl.when(c + 1 < n_col)(lambda: raw_copy(g, True, q).wait_send())
                pl.when((s == 0) & (c > 0))(lambda: raw_copy(g, False, q).wait_send())
            else:
                pl.when(c > 0)(lambda: raw_copy(g, False, q).wait_send())
            each(1, n_row, lambda k: tile_copy(g, k, p, q).wait_send())
        each(0, PIECES, lambda q: sides(s, lambda g, up: one(g, up, q)))

    each(0, n_col, sent)
    each(1, n_row, lambda k: note_copy(k, p).wait_send())
    each(1, n_col, lambda k: line_copy(k, c).wait_send())
    each(1, n_col, lambda k: words_copy(k, c).wait_send())


def fused(n_row, n_col, affiliation, wanted_tiles, slot_peers, edge_words):
    own_rows, community = affiliation.shape
    neg_weight = NEG_RATE * NBR * TILE / (own_rows * n_row * n_col)
    wanted = wanted_tiles.reshape(n_row, 1)
    peers = slot_peers.reshape(NBR, -1)
    words = edge_words.reshape(NBR, TILE // 8, -1)
    note_rows = -(-(n_row + community // 128) // 8) * 8
    dense = n_row * TILE
    width = community // PIECES
    dma = pltpu.SemaphoreType.DMA
    vmem = pl.BlockSpec(memory_space=pltpu.VMEM)
    return pl.pallas_call(
        functools.partial(step_kernel, n_row, n_col, neg_weight),
        out_shape=jax.ShapeDtypeStruct((own_rows, community), jnp.float32),
        in_specs=[pl.BlockSpec(memory_space=pltpu.SMEM), vmem, vmem, vmem],
        out_specs=vmem,
        scratch_shapes=[
            pltpu.VMEM((n_col, PIECES, own_rows, width), jnp.bfloat16),
            pltpu.VMEM((n_col, PIECES, n_row, TILE, width), jnp.bfloat16),
            pltpu.VMEM((n_col, PIECES, dense, width), jnp.bfloat16),
            pltpu.VMEM((n_col, dense // 8, own_rows), jnp.bfloat16),
            pltpu.VMEM((n_col, dense // 8, own_rows), jnp.bfloat16),
            pltpu.VMEM((dense // 8, own_rows), jnp.int32),
            pltpu.VMEM((dense, own_rows), jnp.bfloat16),
            pltpu.VMEM((own_rows, community), jnp.float32),
            pltpu.VMEM((note_rows, 128), jnp.float32),
            pltpu.VMEM((n_row, note_rows, 128), jnp.float32),
            pltpu.VMEM((note_rows, 128), jnp.float32),
            pltpu.VMEM((n_col, note_rows, 128), jnp.float32),
            dma((2, n_col, PIECES)), dma((n_col, PIECES)),
            dma((n_col, PIECES, n_row)), dma((n_col, PIECES, n_row)),
            dma((n_col,)), dma((n_col,)),
            dma((n_row,)), dma((n_row,)),
            dma((n_col,)), dma((n_col,)),
        ],
        compiler_params=pltpu.CompilerParams(
            collective_id=0, has_side_effects=True, vmem_limit_bytes=56 * 2**20),
    )(peers, wanted, affiliation, words)


def fits(n_row, n_col, own_rows, community):
    tile_bytes = 2 * TILE * community * 2 * n_row * n_col
    return n_row & (n_row - 1) == 0 and tile_bytes + 2 * own_rows * community * n_col < 16 * 2**20


def solution(mesh):
    n_row, n_col = mesh.shape["row"], mesh.shape["col"]

    def part(affiliation, *rest):
        if fits(n_row, n_col, *affiliation.shape):
            return fused(n_row, n_col, affiliation, *rest)
        return local(affiliation, *rest)

    in_specs = (
        P(("row", "col"), None),
        P("col", None, "row"),
        P("col", None, "row"),
        P("col", None, None, "row"),
    )
    out_specs = P(("row", "col"), None)
    return jax.shard_map(part, mesh=mesh, in_specs=in_specs, out_specs=out_specs, check_vma=False)
```

```python
import functools
import math

import jax
import jax.numpy as jnp
from jax import lax
from jax.experimental import pallas as pl
from jax.experimental.pallas import tpu as pltpu
from jax.sharding import PartitionSpec as P

TILE = 128
NBR = 8
PIECES = 2
MESH = pl.DeviceIdType.MESH


BACKGROUND = 0.25
NEG_RATE = 0.1
STEP_SIZE = 0.005


def unpack(mask_words):
    shifts = jnp.arange(8, dtype=jnp.int32)
    arc_bits = jnp.bitwise_and(jnp.right_shift(mask_words[..., :, None, :], shifts[:, None]), 1)
    return arc_bits.reshape(
        mask_words.shape[:-2] + (mask_words.shape[-2] * 8, mask_words.shape[-1])
    )


def local(affiliation, wanted_tiles, slot_peers, edge_words):
    own_rows, community = affiliation.shape
    rows_axis = lax.axis_size("row")
    cols_axis = lax.axis_size("col")
    node_count = own_rows * rows_axis * cols_axis
    neg_weight = NEG_RATE * NBR * TILE / node_count
    own_tiles = own_rows // TILE
    range_rows = lax.all_gather(affiliation, "col", axis=0, tiled=True)
    requests = wanted_tiles.reshape(rows_axis)
    group_rows = lax.all_gather(affiliation, "row", axis=0, tiled=True)
    fetched = group_rows.reshape(rows_axis, own_tiles, TILE, community)[
        jnp.arange(rows_axis), requests
    ]
    column_sums = lax.psum(jnp.sum(affiliation, axis=0, dtype=jnp.float32), ("row", "col"))
    peer_table = slot_peers.reshape(NBR, -1)
    word_table = edge_words.reshape(NBR, TILE // 8, -1)
    row_tiles = range_rows.reshape(-1, TILE, community)
    row_count = own_rows * lax.axis_size("col")
    block_tiles = math.gcd(4, row_count // TILE)

    def one_block(block_index):
        start_tile = block_index * block_tiles
        row_block = lax.dynamic_slice_in_dim(row_tiles, start_tile, block_tiles, 0)
        peer_ids = lax.dynamic_slice_in_dim(peer_table, start_tile, block_tiles, 1)
        col_block = fetched[peer_ids]
        mask_words = lax.dynamic_slice_in_dim(word_table, start_tile * TILE, block_tiles * TILE, 2)
        arc_bits = unpack(mask_words).reshape(NBR, TILE, block_tiles, TILE).astype(jnp.float32)
        scores = (
            jnp.einsum("jbvk,buk->jvbu", col_block, row_block, preferred_element_type=jnp.float32)
            / community
            + BACKGROUND
        )
        weights = (arc_bits * (1.0 / jnp.expm1(scores) + neg_weight)).astype(jnp.bfloat16)
        attract = jnp.einsum(
            "jvbu,jbvk->buk", weights, col_block, preferred_element_type=jnp.float32
        )
        return attract.reshape(block_tiles * TILE, community)

    blocks_out = lax.map(one_block, jnp.arange(row_count // (block_tiles * TILE), dtype=jnp.int32))
    merged = lax.psum_scatter(
        blocks_out.reshape(row_count, community), "col", scatter_dimension=0, tiled=True
    )
    own_values = affiliation.astype(jnp.float32)
    gradient = merged - neg_weight * (column_sums[None, :] - own_values)
    return jnp.maximum(own_values + STEP_SIZE * gradient, 0.0)

def step_kernel(
    n_row, n_col, neg_weight,
    peers_ref, wanted_ref, own_ref, words_hbm, out_ref, words_ref, words_sem,
    raw, stage, tiles, words_out, words_in, word_bits, weights, total,
    note, notes, line_note, line_notes,
    raw_send, raw_recv, tile_send, tile_recv, words_send, words_recv,
    note_send, note_recv, line_send, line_recv,
):
    own_rows, community = own_ref.shape
    own_tiles = own_rows // TILE
    lanes = community // 128
    width = community // PIECES
    p = lax.axis_index("row")
    c = lax.axis_index("col")

    def row_peer(k):
        return lax.rem(p + k, n_row)

    def col_peer(k):
        return lax.rem(c + k, n_col)

    def piece(q):
        return pl.ds(pl.multiple_of(q * width, width), width)

    def raw_copy(g, up, q):
        target = jnp.clip(c + 1, 0, n_col - 1) if up else jnp.maximum(c - 1, 0)
        return pltpu.make_async_remote_copy(
            src_ref=raw.at[g, :, piece(q)], dst_ref=raw.at[g, :, piece(q)],
            send_sem=raw_send.at[int(up), g, q], recv_sem=raw_recv.at[g, q],
            device_id=(p, target), device_id_type=MESH)

    def tile_copy(g, k, slot, q):
        return pltpu.make_async_remote_copy(
            src_ref=stage.at[g, k, :, piece(q)],
            dst_ref=tiles.at[g, pl.ds(pl.multiple_of(slot * TILE, TILE), TILE), piece(q)],
            send_sem=tile_send.at[g, q, k], recv_sem=tile_recv.at[g, q, slot],
            device_id=(row_peer(k), c), device_id_type=MESH)

    def words_copy(k, slot):
        return pltpu.make_async_remote_copy(
            src_ref=words_out.at[k], dst_ref=words_in.at[slot],
            send_sem=words_send.at[k], recv_sem=words_recv.at[slot],
            device_id=(p, col_peer(k)), device_id_type=MESH)

    def note_copy(k, slot):
        return pltpu.make_async_remote_copy(
            src_ref=note, dst_ref=notes.at[slot],
            send_sem=note_send.at[k], recv_sem=note_recv.at[slot],
            device_id=(row_peer(k), c), device_id_type=MESH)

    def line_copy(k, slot):
        return pltpu.make_async_remote_copy(
            src_ref=line_note, dst_ref=line_notes.at[slot],
            send_sem=line_send.at[k], recv_sem=line_recv.at[slot],
            device_id=(p, col_peer(k)), device_id_type=MESH)

    def each(first, last, body):
        def step(i, carry):
            body(i)
            return carry
        lax.fori_loop(first, last, step, 0)

    words_fetch = pltpu.make_async_copy(words_hbm, words_ref, words_sem)
    words_fetch.start()
    barrier = pltpu.get_barrier_semaphore()
    for k in range(1, n_row):
        pl.semaphore_signal(barrier, inc=1, device_id=(row_peer(k), c), device_id_type=MESH)
    for k in range(1, n_col):
        pl.semaphore_signal(barrier, inc=1, device_id=(p, col_peer(k)), device_id_type=MESH)

    raw[c] = own_ref[...]
    total[...] = jnp.zeros_like(total)
    sums = jnp.sum(own_ref[...].astype(jnp.float32), axis=0, keepdims=True)
    note[...] = jnp.zeros_like(note)
    for i in range(n_row):
        note[pl.ds(i, 1), :] = jnp.full((1, 128), wanted_ref[i], jnp.int32).astype(jnp.float32)
    for i in range(lanes):
        note[pl.ds(n_row + i, 1), :] = sums[:, i * 128:(i + 1) * 128]
    notes[p] = note[...]
    pl.semaphore_wait(barrier, n_row - 1 + n_col - 1)

    each(1, n_row, lambda k: note_copy(k, p).start())

    def send_own(q):
        pl.when(c + 1 < n_col)(lambda: raw_copy(c, True, q).start())
        pl.when(c > 0)(lambda: raw_copy(c, False, q).start())

    each(0, PIECES, send_own)

    def order_words(k):
        b = col_peer(k)
        for t in range(own_tiles):
            at = b * own_tiles + t
            lane = pl.ds(pl.multiple_of(at * TILE, TILE), TILE)
            slot_words = [words_ref[j, :, lane] for j in range(NBR)]
            slot_peer = [peers_ref[j, at] for j in range(NBR)]
            for q in range(n_row):
                got = jnp.zeros((TILE // 8, TILE), jnp.int32)
                for j in range(NBR):
                    got = jnp.where(slot_peer[j] == q, slot_words[j], got)
                words_out[k, q * 16:(q + 1) * 16, t * TILE:(t + 1) * TILE] = (
                    got.astype(jnp.float32).astype(jnp.bfloat16))

    each(1, n_row, lambda k: note_copy(k, row_peer(k)).wait_recv())
    line_note[...] = jnp.sum(notes[...], axis=0)
    for r in range(n_row):
        line_note[pl.ds(r, 1), :] = notes[r, pl.ds(p, 1), :]
    line_notes[c] = line_note[...]
    each(1, n_col, lambda k: line_copy(k, c).start())

    def send_tiles(g, q):
        def pick(k):
            r = row_peer(k)
            wanted = line_notes[g, pl.ds(r, 1), :]
            picks = [
                jnp.broadcast_to(
                    jnp.concatenate([jnp.where(wanted == i, 1.0, 0.0)] * (width // 128), axis=1),
                    (16, width)).astype(jnp.bfloat16)
                for i in range(own_tiles)]
            for h in range(TILE // 16):
                got = raw[g, h * 16:(h + 1) * 16, piece(q)] * picks[0]
                for i in range(1, own_tiles):
                    got = got + raw[g, i * TILE + h * 16:i * TILE + (h + 1) * 16, piece(q)] * picks[i]
                stage[g, k, h * 16:(h + 1) * 16, piece(q)] = got

        def send(k):
            pick(k)
            tile_copy(g, k, p, q).start()

        each(1, n_row, send)
        pick(0)
        tiles[g, pl.ds(pl.multiple_of(p * TILE, TILE), TILE), piece(q)] = stage[g, 0, :, piece(q)]

    chunk = math.gcd(4, n_row) * TILE
    bit_of_row = lax.shift_left(1, lax.broadcasted_iota(jnp.int32, (chunk // 8, 8, own_rows), 1))
    scale = math.log2(math.e)

    def compute(g):
        word_bits[...] = words_in[g].astype(jnp.float32).astype(jnp.int32)

        def part(i):
            rows = pl.ds(pl.multiple_of(i * chunk, chunk), chunk)
            scores = lax.dot_general(
                tiles[g, rows, :], own_ref[...], (((1,), (1,)), ((), ())),
                preferred_element_type=jnp.float32)
            grown = jnp.exp2(scores * (scale / community) + BACKGROUND * scale)
            value = 1.0 / (grown - 1.0) + neg_weight
            words = word_bits[pl.ds(pl.multiple_of(i * (chunk // 8), chunk // 8), chunk // 8), :]
            arcs = jnp.bitwise_and(
                jnp.broadcast_to(words[:, None, :], (chunk // 8, 8, own_rows)), bit_of_row)
            value = jnp.where(arcs.reshape(chunk, own_rows) != 0, value, 0.0)
            weights[rows, :] = value.astype(jnp.bfloat16)

        each(0, n_row * TILE // chunk, part)
        total[...] += lax.dot_general(
            weights[...], tiles[g], (((0,), (0,)), ((), ())),
            preferred_element_type=jnp.float32)

    each(0, PIECES, lambda q: send_tiles(c, q))
    words_fetch.wait()
    each(0, n_col, order_words)
    words_in[c] = words_out[0]
    each(1, n_col, lambda k: words_copy(k, c).start())
    each(1, n_col, lambda k: line_copy(k, col_peer(k)).wait_recv())

    def sides(s, body):
        @pl.when(c - s >= 0)
        def _():
            body(c - s, True)

        @pl.when((s > 0) & (c + s < n_col))
        def _():
            body(c + s, False)

    def arrive(g, up, q):
        raw_copy(g, up, q).wait_recv()
        if up:
            pl.when(c + 1 < n_col)(lambda: raw_copy(g, True, q).start())
        else:
            pl.when(c > 0)(lambda: raw_copy(g, False, q).start())
        send_tiles(g, q)

    def use(g, up):
        each(0, PIECES, lambda q: each(
            1, n_row, lambda k: tile_copy(g, k, row_peer(k), q).wait_recv()))
        pl.when(g != c)(lambda: words_copy(1, g).wait_recv())
        compute(g)

    def step(s):
        each(0, PIECES, lambda q: sides(s, lambda g, up: arrive(g, up, q)))
        sides(s - 1, use)

    each(1, n_col + 1, step)

    sums_all = jnp.sum(line_notes[...], axis=0)
    for i in range(lanes):
        lane = slice(i * 128, (i + 1) * 128)
        own_values = own_ref[:, lane].astype(jnp.float32)
        gradient = total[:, lane] - neg_weight * (sums_all[n_row + i:n_row + i + 1, :] - own_values)
        out_ref[:, lane] = own_values + STEP_SIZE * gradient

    def sent(s):
        def one(g, up, q):
            if up:
                pl.when(c + 1 < n_col)(lambda: raw_copy(g, True, q).wait_send())
                pl.when((s == 0) & (c > 0))(lambda: raw_copy(g, False, q).wait_send())
            else:
                pl.when(c > 0)(lambda: raw_copy(g, False, q).wait_send())
            each(1, n_row, lambda k: tile_copy(g, k, p, q).wait_send())
        each(0, PIECES, lambda q: sides(s, lambda g, up: one(g, up, q)))

    each(0, n_col, sent)
    each(1, n_row, lambda k: note_copy(k, p).wait_send())
    each(1, n_col, lambda k: line_copy(k, c).wait_send())
    each(1, n_col, lambda k: words_copy(k, c).wait_send())


def fused(n_row, n_col, affiliation, wanted_tiles, slot_peers, edge_words):
    own_rows, community = affiliation.shape
    neg_weight = NEG_RATE * NBR * TILE / (own_rows * n_row * n_col)
    wanted = wanted_tiles.reshape(n_row)
    peers = slot_peers.reshape(NBR, -1)
    words = edge_words.reshape(NBR, TILE // 8, -1)
    note_rows = -(-(n_row + community // 128) // 8) * 8
    dense = n_row * TILE
    dma = pltpu.SemaphoreType.DMA
    vmem = pl.BlockSpec(memory_space=pltpu.VMEM)
    smem = pl.BlockSpec(memory_space=pltpu.SMEM)
    moved = pl.pallas_call(
        functools.partial(step_kernel, n_row, n_col, neg_weight),
        out_shape=jax.ShapeDtypeStruct((own_rows, community), jnp.float32),
        in_specs=[smem, smem, vmem, pl.BlockSpec(memory_space=pl.ANY)],
        out_specs=vmem,
        scratch_shapes=[
            pltpu.VMEM(words.shape, jnp.int32), dma,
            pltpu.VMEM((n_col, own_rows, community), jnp.bfloat16),
            pltpu.VMEM((n_col, n_row, TILE, community), jnp.bfloat16),
            pltpu.VMEM((n_col, dense, community), jnp.bfloat16),
            pltpu.VMEM((n_col, dense // 8, own_rows), jnp.bfloat16),
            pltpu.VMEM((n_col, dense // 8, own_rows), jnp.bfloat16),
            pltpu.VMEM((dense // 8, own_rows), jnp.int32),
            pltpu.VMEM((dense, own_rows), jnp.bfloat16),
            pltpu.VMEM((own_rows, community), jnp.float32),
            pltpu.VMEM((note_rows, 128), jnp.float32),
            pltpu.VMEM((n_row, note_rows, 128), jnp.float32),
            pltpu.VMEM((note_rows, 128), jnp.float32),
            pltpu.VMEM((n_col, note_rows, 128), jnp.float32),
            dma((2, n_col, PIECES)), dma((n_col, PIECES)),
            dma((n_col, PIECES, n_row)), dma((n_col, PIECES, n_row)),
            dma((n_col,)), dma((n_col,)),
            dma((n_row,)), dma((n_row,)),
            dma((n_col,)), dma((n_col,)),
        ],
        compiler_params=pltpu.CompilerParams(
            collective_id=0, has_side_effects=True, vmem_limit_bytes=56 * 2**20),
    )(peers, wanted, affiliation, words)
    return jnp.maximum(moved, 0.0)


def fits(n_row, n_col, own_rows, community):
    tile_bytes = 2 * TILE * community * 2 * n_row * n_col
    return tile_bytes + 2 * own_rows * community * n_col < 16 * 2**20


def solution(mesh):
    n_row, n_col = mesh.shape["row"], mesh.shape["col"]

    def part(affiliation, *rest):
        if fits(n_row, n_col, *affiliation.shape):
            return fused(n_row, n_col, affiliation, *rest)
        return local(affiliation, *rest)

    in_specs = (
        P(("row", "col"), None),
        P("col", None, "row"),
        P("col", None, "row"),
        P("col", None, None, "row"),
    )
    out_specs = P(("row", "col"), None)
    return jax.shard_map(part, mesh=mesh, in_specs=in_specs, out_specs=out_specs, check_vma=False)
```

```python
import functools
import math

import jax
import jax.numpy as jnp
from jax import lax
from jax.experimental import pallas as pl
from jax.experimental.pallas import tpu as pltpu
from jax.sharding import PartitionSpec as P

TILE = 128
NBR = 8
PIECES = 2
MESH = pl.DeviceIdType.MESH


BACKGROUND = 0.25
NEG_RATE = 0.1
STEP_SIZE = 0.005


def unpack(mask_words):
    shifts = jnp.arange(8, dtype=jnp.int32)
    arc_bits = jnp.bitwise_and(jnp.right_shift(mask_words[..., :, None, :], shifts[:, None]), 1)
    return arc_bits.reshape(
        mask_words.shape[:-2] + (mask_words.shape[-2] * 8, mask_words.shape[-1])
    )


def local(affiliation, wanted_tiles, slot_peers, edge_words):
    own_rows, community = affiliation.shape
    rows_axis = lax.axis_size("row")
    cols_axis = lax.axis_size("col")
    node_count = own_rows * rows_axis * cols_axis
    neg_weight = NEG_RATE * NBR * TILE / node_count
    own_tiles = own_rows // TILE
    range_rows = lax.all_gather(affiliation, "col", axis=0, tiled=True)
    requests = wanted_tiles.reshape(rows_axis)
    group_rows = lax.all_gather(affiliation, "row", axis=0, tiled=True)
    fetched = group_rows.reshape(rows_axis, own_tiles, TILE, community)[
        jnp.arange(rows_axis), requests
    ]
    column_sums = lax.psum(jnp.sum(affiliation, axis=0, dtype=jnp.float32), ("row", "col"))
    peer_table = slot_peers.reshape(NBR, -1)
    word_table = edge_words.reshape(NBR, TILE // 8, -1)
    row_tiles = range_rows.reshape(-1, TILE, community)
    row_count = own_rows * lax.axis_size("col")
    block_tiles = math.gcd(4, row_count // TILE)

    def one_block(block_index):
        start_tile = block_index * block_tiles
        row_block = lax.dynamic_slice_in_dim(row_tiles, start_tile, block_tiles, 0)
        peer_ids = lax.dynamic_slice_in_dim(peer_table, start_tile, block_tiles, 1)
        col_block = fetched[peer_ids]
        mask_words = lax.dynamic_slice_in_dim(word_table, start_tile * TILE, block_tiles * TILE, 2)
        arc_bits = unpack(mask_words).reshape(NBR, TILE, block_tiles, TILE).astype(jnp.float32)
        scores = (
            jnp.einsum("jbvk,buk->jvbu", col_block, row_block, preferred_element_type=jnp.float32)
            / community
            + BACKGROUND
        )
        weights = (arc_bits * (1.0 / jnp.expm1(scores) + neg_weight)).astype(jnp.bfloat16)
        attract = jnp.einsum(
            "jvbu,jbvk->buk", weights, col_block, preferred_element_type=jnp.float32
        )
        return attract.reshape(block_tiles * TILE, community)

    blocks_out = lax.map(one_block, jnp.arange(row_count // (block_tiles * TILE), dtype=jnp.int32))
    merged = lax.psum_scatter(
        blocks_out.reshape(row_count, community), "col", scatter_dimension=0, tiled=True
    )
    own_values = affiliation.astype(jnp.float32)
    gradient = merged - neg_weight * (column_sums[None, :] - own_values)
    return jnp.maximum(own_values + STEP_SIZE * gradient, 0.0)

def step_kernel(
    n_row, n_col, neg_weight,
    peers_ref, wanted_ref, own_ref, words_hbm, out_ref, words_ref, words_sem,
    raw, stage, tiles, words_out, words_in, word_bits, weights, total,
    note, notes, line_note, line_notes,
    raw_send, raw_recv, tile_send, tile_recv, words_send, words_recv,
    note_send, note_recv, line_send, line_recv,
):
    own_rows, community = own_ref.shape
    own_tiles = own_rows // TILE
    lanes = community // 128
    width = community // PIECES
    p = lax.axis_index("row")
    c = lax.axis_index("col")

    def row_peer(k):
        return lax.rem(p + k, n_row)

    def col_peer(k):
        return lax.rem(c + k, n_col)

    def piece(q):
        return pl.ds(pl.multiple_of(q * width, width), width)

    def raw_copy(g, up, q):
        target = jnp.clip(c + 1, 0, n_col - 1) if up else jnp.maximum(c - 1, 0)
        return pltpu.make_async_remote_copy(
            src_ref=raw.at[g, :, piece(q)], dst_ref=raw.at[g, :, piece(q)],
            send_sem=raw_send.at[int(up), g, q], recv_sem=raw_recv.at[g, q],
            device_id=(p, target), device_id_type=MESH)

    def tile_copy(g, k, slot, q):
        return pltpu.make_async_remote_copy(
            src_ref=stage.at[g, k, :, piece(q)],
            dst_ref=tiles.at[g, pl.ds(pl.multiple_of(slot * TILE, TILE), TILE), piece(q)],
            send_sem=tile_send.at[g, q, k], recv_sem=tile_recv.at[g, q, slot],
            device_id=(row_peer(k), c), device_id_type=MESH)

    def words_copy(k, slot):
        return pltpu.make_async_remote_copy(
            src_ref=words_out.at[k], dst_ref=words_in.at[slot],
            send_sem=words_send.at[k], recv_sem=words_recv.at[slot],
            device_id=(p, col_peer(k)), device_id_type=MESH)

    def note_copy(k, slot):
        return pltpu.make_async_remote_copy(
            src_ref=note, dst_ref=notes.at[slot],
            send_sem=note_send.at[k], recv_sem=note_recv.at[slot],
            device_id=(row_peer(k), c), device_id_type=MESH)

    def line_copy(k, slot):
        return pltpu.make_async_remote_copy(
            src_ref=line_note, dst_ref=line_notes.at[slot],
            send_sem=line_send.at[k], recv_sem=line_recv.at[slot],
            device_id=(p, col_peer(k)), device_id_type=MESH)

    def each(first, last, body):
        def step(i, carry):
            body(i)
            return carry
        lax.fori_loop(first, last, step, 0)

    words_fetch = pltpu.make_async_copy(words_hbm, words_ref, words_sem)
    words_fetch.start()
    barrier = pltpu.get_barrier_semaphore()
    for k in range(1, n_row):
        pl.semaphore_signal(barrier, inc=1, device_id=(row_peer(k), c), device_id_type=MESH)
    for k in range(1, n_col):
        pl.semaphore_signal(barrier, inc=1, device_id=(p, col_peer(k)), device_id_type=MESH)

    raw[c] = own_ref[...]
    total[...] = jnp.zeros_like(total)
    sums = jnp.sum(own_ref[...].astype(jnp.float32), axis=0, keepdims=True)
    note[...] = jnp.zeros_like(note)
    for i in range(n_row):
        note[pl.ds(i, 1), :] = jnp.full((1, 128), wanted_ref[i], jnp.int32).astype(jnp.float32)
    for i in range(lanes):
        note[pl.ds(n_row + i, 1), :] = sums[:, i * 128:(i + 1) * 128]
    notes[p] = note[...]
    pl.semaphore_wait(barrier, n_row - 1 + n_col - 1)

    each(1, n_row, lambda k: note_copy(k, p).start())

    def send_own(q):
        pl.when(c + 1 < n_col)(lambda: raw_copy(c, True, q).start())
        pl.when(c > 0)(lambda: raw_copy(c, False, q).start())

    each(0, PIECES, send_own)

    def order_words(k):
        b = col_peer(k)
        for t in range(own_tiles):
            at = b * own_tiles + t
            lane = pl.ds(pl.multiple_of(at * TILE, TILE), TILE)
            slot_words = [words_ref[j, :, lane] for j in range(NBR)]
            slot_peer = [peers_ref[j, at] for j in range(NBR)]
            for q in range(n_row):
                got = jnp.zeros((TILE // 8, TILE), jnp.int32)
                for j in range(NBR):
                    got = jnp.where(slot_peer[j] == q, slot_words[j], got)
                words_out[k, q * 16:(q + 1) * 16, t * TILE:(t + 1) * TILE] = (
                    got.astype(jnp.float32).astype(jnp.bfloat16))

    each(1, n_row, lambda k: note_copy(k, row_peer(k)).wait_recv())
    line_note[...] = jnp.sum(notes[...], axis=0)
    for r in range(n_row):
        line_note[pl.ds(r, 1), :] = notes[r, pl.ds(p, 1), :]
    line_notes[c] = line_note[...]
    each(1, n_col, lambda k: line_copy(k, c).start())

    def send_tiles(g, q):
        def pick(k):
            r = row_peer(k)
            wanted = line_notes[g, pl.ds(r, 1), :]
            picks = [
                jnp.broadcast_to(
                    jnp.concatenate([jnp.where(wanted == i, 1.0, 0.0)] * (width // 128), axis=1),
                    (16, width)).astype(jnp.bfloat16)
                for i in range(own_tiles)]
            for h in range(TILE // 16):
                got = raw[g, h * 16:(h + 1) * 16, piece(q)] * picks[0]
                for i in range(1, own_tiles):
                    got = got + raw[g, i * TILE + h * 16:i * TILE + (h + 1) * 16, piece(q)] * picks[i]
                stage[g, k, h * 16:(h + 1) * 16, piece(q)] = got

        def send(k):
            pick(k)
            tile_copy(g, k, p, q).start()

        each(1, n_row, send)
        pick(0)
        tiles[g, pl.ds(pl.multiple_of(p * TILE, TILE), TILE), piece(q)] = stage[g, 0, :, piece(q)]

    chunk = math.gcd(4, n_row) * TILE
    parts = n_row * TILE // chunk
    bit_of_row = lax.shift_left(1, lax.broadcasted_iota(jnp.int32, (chunk // 8, 8, own_rows), 1))
    scale = math.log2(math.e)

    def compute(g):
        word_bits[...] = words_in[g].astype(jnp.float32).astype(jnp.int32)

        def part(step):
            i = lax.rem(lax.div(p, chunk // TILE) + step, parts)
            for j in range(chunk // TILE):
                slot = i * (chunk // TILE) + j
                pl.when(slot != p)(lambda slot=slot: each(
                    0, PIECES, lambda q: tile_copy(g, 1, slot, q).wait_recv()))
            rows = pl.ds(pl.multiple_of(i * chunk, chunk), chunk)
            scores = lax.dot_general(
                tiles[g, rows, :], own_ref[...], (((1,), (1,)), ((), ())),
                preferred_element_type=jnp.float32)
            grown = jnp.exp2(scores * (scale / community) + BACKGROUND * scale)
            value = 1.0 / (grown - 1.0) + neg_weight
            words = word_bits[pl.ds(pl.multiple_of(i * (chunk // 8), chunk // 8), chunk // 8), :]
            arcs = jnp.bitwise_and(
                jnp.broadcast_to(words[:, None, :], (chunk // 8, 8, own_rows)), bit_of_row)
            value = jnp.where(arcs.reshape(chunk, own_rows) != 0, value, 0.0)
            weights[rows, :] = value.astype(jnp.bfloat16)

        each(0, parts, part)
        total[...] += lax.dot_general(
            weights[...], tiles[g], (((0,), (0,)), ((), ())),
            preferred_element_type=jnp.float32)

    each(0, PIECES, lambda q: send_tiles(c, q))
    words_fetch.wait()
    each(0, n_col, order_words)
    words_in[c] = words_out[0]
    each(1, n_col, lambda k: words_copy(k, c).start())
    each(1, n_col, lambda k: line_copy(k, col_peer(k)).wait_recv())

    def sides(s, body):
        @pl.when(c - s >= 0)
        def _():
            body(c - s, True)

        @pl.when((s > 0) & (c + s < n_col))
        def _():
            body(c + s, False)

    def arrive(g, up, q):
        raw_copy(g, up, q).wait_recv()
        if up:
            pl.when(c + 1 < n_col)(lambda: raw_copy(g, True, q).start())
        else:
            pl.when(c > 0)(lambda: raw_copy(g, False, q).start())
        send_tiles(g, q)

    def use(g, up):
        pl.when(g != c)(lambda: words_copy(1, g).wait_recv())
        compute(g)

    def step(s):
        each(0, PIECES, lambda q: sides(s, lambda g, up: arrive(g, up, q)))
        sides(s - 1, use)

    each(1, n_col + 1, step)

    sums_all = jnp.sum(line_notes[...], axis=0)
    for i in range(lanes):
        lane = slice(i * 128, (i + 1) * 128)
        own_values = own_ref[:, lane].astype(jnp.float32)
        gradient = total[:, lane] - neg_weight * (sums_all[n_row + i:n_row + i + 1, :] - own_values)
        out_ref[:, lane] = own_values + STEP_SIZE * gradient

    def sent(s):
        def one(g, up, q):
            if up:
                pl.when(c + 1 < n_col)(lambda: raw_copy(g, True, q).wait_send())
                pl.when((s == 0) & (c > 0))(lambda: raw_copy(g, False, q).wait_send())
            else:
                pl.when(c > 0)(lambda: raw_copy(g, False, q).wait_send())
            each(1, n_row, lambda k: tile_copy(g, k, p, q).wait_send())
        each(0, PIECES, lambda q: sides(s, lambda g, up: one(g, up, q)))

    each(0, n_col, sent)
    each(1, n_row, lambda k: note_copy(k, p).wait_send())
    each(1, n_col, lambda k: line_copy(k, c).wait_send())
    each(1, n_col, lambda k: words_copy(k, c).wait_send())


def fused(n_row, n_col, affiliation, wanted_tiles, slot_peers, edge_words):
    own_rows, community = affiliation.shape
    neg_weight = NEG_RATE * NBR * TILE / (own_rows * n_row * n_col)
    wanted = wanted_tiles.reshape(n_row)
    peers = slot_peers.reshape(NBR, -1)
    words = edge_words.reshape(NBR, TILE // 8, -1)
    note_rows = -(-(n_row + community // 128) // 8) * 8
    dense = n_row * TILE
    dma = pltpu.SemaphoreType.DMA
    vmem = pl.BlockSpec(memory_space=pltpu.VMEM)
    smem = pl.BlockSpec(memory_space=pltpu.SMEM)
    moved = pl.pallas_call(
        functools.partial(step_kernel, n_row, n_col, neg_weight),
        out_shape=jax.ShapeDtypeStruct((own_rows, community), jnp.float32),
        in_specs=[smem, smem, vmem, pl.BlockSpec(memory_space=pl.ANY)],
        out_specs=vmem,
        scratch_shapes=[
            pltpu.VMEM(words.shape, jnp.int32), dma,
            pltpu.VMEM((n_col, own_rows, community), jnp.bfloat16),
            pltpu.VMEM((n_col, n_row, TILE, community), jnp.bfloat16),
            pltpu.VMEM((n_col, dense, community), jnp.bfloat16),
            pltpu.VMEM((n_col, dense // 8, own_rows), jnp.bfloat16),
            pltpu.VMEM((n_col, dense // 8, own_rows), jnp.bfloat16),
            pltpu.VMEM((dense // 8, own_rows), jnp.int32),
            pltpu.VMEM((dense, own_rows), jnp.bfloat16),
            pltpu.VMEM((own_rows, community), jnp.float32),
            pltpu.VMEM((note_rows, 128), jnp.float32),
            pltpu.VMEM((n_row, note_rows, 128), jnp.float32),
            pltpu.VMEM((note_rows, 128), jnp.float32),
            pltpu.VMEM((n_col, note_rows, 128), jnp.float32),
            dma((2, n_col, PIECES)), dma((n_col, PIECES)),
            dma((n_col, PIECES, n_row)), dma((n_col, PIECES, n_row)),
            dma((n_col,)), dma((n_col,)),
            dma((n_row,)), dma((n_row,)),
            dma((n_col,)), dma((n_col,)),
        ],
        compiler_params=pltpu.CompilerParams(
            collective_id=0, has_side_effects=True, vmem_limit_bytes=56 * 2**20),
    )(peers, wanted, affiliation, words)
    return jnp.maximum(moved, 0.0)


def fits(n_row, n_col, own_rows, community):
    tile_bytes = 2 * TILE * community * 2 * n_row * n_col
    return tile_bytes + 2 * own_rows * community * n_col < 16 * 2**20


def solution(mesh):
    n_row, n_col = mesh.shape["row"], mesh.shape["col"]

    def part(affiliation, *rest):
        if fits(n_row, n_col, *affiliation.shape):
            return fused(n_row, n_col, affiliation, *rest)
        return local(affiliation, *rest)

    in_specs = (
        P(("row", "col"), None),
        P("col", None, "row"),
        P("col", None, "row"),
        P("col", None, None, "row"),
    )
    out_specs = P(("row", "col"), None)
    return jax.shard_map(part, mesh=mesh, in_specs=in_specs, out_specs=out_specs, check_vma=False)
```
